32 devices in a mesh: grp: 2 (over y), pair: 8 (over z, core), seg: 2 (over x), lag: 1.
Axes of the slice: x: 2, y: 2, z: 4, core: 2. Of those that a mesh axis runs over, the one named last changes fastest.
Arguments:
- strain: float32 [4096, 1024], P(('grp', 'pair'), 'seg'), parts along dimension 0, may hold values from -1000 to 1000, as said below
- block_slot: int32 [32], P('grp'), parts along dimension 0, may hold values from 0 to 15, as said below
- pair_blocks: int32 [128, 2], P('grp'), parts along dimension 0, may hold values from 0 to 15, as said below
Outputs:
- stacks: float32 [128, 400, 128], P(('grp', 'pair', 'seg'), 'lag'), parts along dimension 0
The draws below stay inside these ranges and needn't reach their ends.
There are 2 independent parts, one for each index of `grp`. The reference program is written for one: setup_inputs(seed, part) draws one part's arguments, and reference() takes and returns one part's arrays. A program takes and returns all parts, laid end to end along the dimension named above; each array names one. Nothing has to cross between parts.
Inputs may be any that keep to these rules, and one draw needn't show every extreme that they name: A permutation; block b is held by index block_slot[b] // 2 of pair. `pair_blocks`: rows p * 8 to (p + 1) * 8 - 1 are the pairs of index p of pair; together they name 16 distinct blocks; no index of pair holds more than 2 of them, and some index holds exactly 2. `strain`: channel gains and envelopes differ widely.
All inputs are finite; a program needn't handle non-finite values.
Results may differ from the reference program's by a relative error of at most 0.006.
Values may be sent and summed in bfloat16 or wider, within the bound.
A program may use at most 64 MiB of HBM per device.

```python
import math
import jax
import jax.numpy as jnp
from jax import lax

CHB = 128
WIN = 512
MAXLAG = 200
HALF = 64
BLK_DEV = 2
PAIRS_DEV = 8
LAGS = 400
NSEG = 2
NBLK = 16
CHANNELS = 2048
NPAIRS = 64
CAP = 2
N_PAIR = 8


def slot_table(key):
    return jax.random.permutation(key, NBLK).astype(jnp.int32)


def draw_block_slot(key, part):
    slots = slot_table(key)
    return slots


def draw_pair_blocks(key, part):
    slots = slot_table(key)
    key = jax.random.fold_in(key, 7)
    inverse = jnp.zeros((NBLK,), jnp.int32).at[slots].set(jnp.arange(NBLK, dtype=jnp.int32))

    def one_device(index):
        sub_key = jax.random.fold_in(key, index)
        cells = jax.random.permutation(jax.random.fold_in(sub_key, 1), N_PAIR * CAP)[:2 * PAIRS_DEV]
        owners = cells // CAP
        ranks = cells % CAP
        offset = jax.random.randint(jax.random.fold_in(sub_key, 2), (N_PAIR,), 0, BLK_DEV)
        local = (ranks + offset[owners]) % BLK_DEV
        return inverse[owners * BLK_DEV + local]
    table = jax.vmap(one_device)(jnp.arange(N_PAIR, dtype=jnp.int32))
    return table.reshape(NPAIRS, 2).astype(jnp.int32)


def draw_strain(key, part):
    key = jax.random.fold_in(key, 11)
    noise_key, gain_key, envelope_key = jax.random.split(key, 3)
    shape = (CHANNELS, NSEG * WIN // 16, 16)
    noise = jnp.clip(jax.random.normal(noise_key, shape, jnp.float32), -6.0, 6.0)
    top = math.log(10.0)
    gains = jnp.exp(jax.random.uniform(gain_key, (CHANNELS, 1, 1), jnp.float32, 0.0, top))
    envelope = jnp.exp(jax.random.uniform(envelope_key, (CHANNELS, NSEG * WIN // 16, 1), jnp.float32, 0.0, top))
    return (noise * gains * envelope).reshape(CHANNELS, NSEG * WIN).astype(jnp.float32)


def setup_inputs(seed: int = 0, part: int = 0) -> dict:
    arg_keys = jax.random.split(jax.random.key(seed), 4)
    part_splits = jax.random.split(jax.random.fold_in(arg_keys[3], part), 4)
    return {
        "strain": draw_strain(jax.random.fold_in(jax.random.fold_in(arg_keys[3], part), 71), part),
        "block_slot": draw_block_slot(jax.random.fold_in(jax.random.fold_in(arg_keys[3], part), 71), part),
        "pair_blocks": draw_pair_blocks(jax.random.fold_in(jax.random.fold_in(arg_keys[3], part), 71), part),
    }


EPS = 1e-06

def reference(strain, block_slot, pair_blocks):
    series = strain.reshape(CHANNELS, NSEG, WIN)
    magnitude = jnp.abs(series)
    padded = jnp.pad(magnitude, ((0, 0), (0, 0), (HALF, HALF)))
    running = jnp.cumsum(padded, axis=2)
    running = jnp.concatenate([jnp.zeros((CHANNELS, NSEG, 1), running.dtype), running], axis=2)
    sums = running[:, :, 2 * HALF + 1:] - running[:, :, :WIN]
    times = jnp.arange(WIN, dtype=jnp.int32)
    count = (jnp.minimum(times + HALF, WIN - 1) - jnp.maximum(times - HALF, 0) + 1).astype(jnp.float32)
    normed = (series / (sums / count + EPS)).astype(jnp.bfloat16)
    blocks = normed.reshape(NBLK, CHB, NSEG, WIN)
    slots = block_slot[pair_blocks].astype(jnp.int32)
    scale = 1.0 / math.sqrt(NSEG * WIN)
    shifts = (jnp.arange(LAGS, dtype=jnp.int32) - MAXLAG) % (2 * WIN)

    def one_pair(pair_slots):
        first = blocks[pair_slots[0]].astype(jnp.float32)
        second = blocks[pair_slots[1]].astype(jnp.float32)
        first_f = jnp.fft.rfft(first, n=2 * WIN, axis=-1)
        second_f = jnp.fft.rfft(second, n=2 * WIN, axis=-1)
        cross = lax.optimization_barrier(jnp.sum(jnp.conj(first_f) * second_f, axis=1))
        full = jnp.fft.irfft(cross, n=2 * WIN, axis=-1)
        return jnp.transpose(full[:, shifts] * scale)
    return lax.map(one_pair, slots)
```

```python
import functools
import math

import jax
import jax.numpy as jnp
import numpy as np
from jax import lax
from jax.experimental import pallas as pl
from jax.experimental.pallas import tpu as pltpu
from jax.sharding import PartitionSpec as P

CHB = 128
WIN = 512
MAXLAG = 200
HALF = 64
LAGS = 400


EPS = 1e-06


def make_tables(freq_part, lag_count):
    half_bins = WIN // lag_count
    length = 2 * WIN
    freq = freq_part * half_bins + jnp.arange(half_bins, dtype=jnp.int32)
    times = jnp.arange(WIN, dtype=jnp.int32)
    first_bin = freq == 0
    angle = (times[:, None] * freq[None, :] % length).astype(jnp.float32) * (2.0 * math.pi / length)
    alternate = (1 - 2 * (times % 2)).astype(jnp.float32)
    sine = jnp.where(first_bin[None, :], alternate[:, None], jnp.sin(angle))
    forward = jnp.concatenate([jnp.cos(angle), sine], axis=1)
    forward_high = forward.astype(jnp.bfloat16)
    forward_low = (forward - forward_high.astype(jnp.float32)).astype(jnp.bfloat16)
    shifts = jnp.arange(LAGS, dtype=jnp.int32) - MAXLAG
    back_angle = (freq[:, None] * shifts[None, :] % length).astype(jnp.float32) * (
        2.0 * math.pi / length
    )
    weight = jnp.where(first_bin, 1.0, 2.0).astype(jnp.float32)[:, None]
    upper = weight * jnp.cos(back_angle) / length
    lag_sign = (1 - 2 * (shifts % 2)).astype(jnp.float32)
    lower = jnp.where(
        first_bin[:, None], lag_sign[None, :] / length, -2.0 * jnp.sin(back_angle) / length
    )
    inverse = jnp.concatenate([upper, lower], axis=0)
    keep = (freq > 0).astype(jnp.float32)
    return ((forward_high, forward_low), inverse, keep)


def spectra(blocks, tables):
    high = jnp.einsum("bcst,tk->bcsk", blocks, tables[0], preferred_element_type=jnp.float32)
    low = jnp.einsum("bcst,tk->bcsk", blocks, tables[1], preferred_element_type=jnp.float32)
    return high + low


def cross_stack(first, second, keep, half_bins):
    first_re, first_im = (first[..., :half_bins], first[..., half_bins:])
    second_re, second_im = (second[..., :half_bins], second[..., half_bins:])
    real_part = first_re * second_re + keep * first_im * second_im
    imag_part = (
        keep * (first_im * second_re - first_re * second_im) + (1.0 - keep) * first_im * second_im
    )
    return jnp.sum(jnp.concatenate([real_part, imag_part], axis=-1), axis=2)


def to_lags(cross, inverse):
    return jnp.einsum("pck,kl->plc", cross, inverse, precision=lax.Precision.HIGHEST)


def shards(strain, block_slot, pair_blocks):
    pair_count = lax.axis_size("pair")
    seg_count = lax.axis_size("seg")
    lag_count = lax.axis_size("lag")
    holder = lax.axis_index("pair")
    freq_part = lax.axis_index("lag")
    blk_dev = strain.shape[0] // CHB
    seg_dev = strain.shape[1] // WIN
    nblk = block_slot.shape[0]
    pairs_dev = pair_blocks.shape[0] // pair_count
    refs = 2 * pairs_dev
    capacity = (refs + pair_count - 1) // pair_count
    half_bins = WIN // lag_count
    scale = 1.0 / math.sqrt(seg_dev * seg_count * WIN)
    series = strain.reshape(blk_dev, CHB, seg_dev, WIN)
    times = jnp.arange(WIN, dtype=jnp.int32)
    band = (jnp.abs(times[:, None] - times[None, :]) <= HALF).astype(jnp.float32)
    count = jnp.sum(band, axis=0)
    sums = jnp.einsum("bcst,tu->bcsu", jnp.abs(series), band, precision=lax.Precision.HIGHEST)
    normed = (series / (sums / count + EPS)).astype(jnp.bfloat16)
    tables, inverse, keep = make_tables(freq_part, lag_count)
    catalog = jnp.arange(nblk, dtype=jnp.int32)
    wanted = pair_blocks.reshape(pair_count, refs)
    hits = (wanted[:, :, None] == catalog[None, None, :]).astype(jnp.int32)
    ref_slot = jnp.sum(hits * block_slot[None, None, :], axis=2)
    ref_owner = ref_slot // blk_dev
    ref_local = ref_slot % blk_dev
    ordering = jnp.arange(refs, dtype=jnp.int32)
    earlier = ordering[:, None] > ordering[None, :]
    ref_rank = jnp.sum(
        ((ref_owner[:, :, None] == ref_owner[:, None, :]) & earlier[None, :, :]).astype(jnp.int32),
        axis=2,
    )
    mine = ref_owner == holder
    rank_hot = (
        (ref_rank[:, :, None] == jnp.arange(capacity, dtype=jnp.int32)[None, None, :])
        & mine[:, :, None]
    ).astype(jnp.float32)
    local_hot = (
        ref_local[:, :, None] == jnp.arange(blk_dev, dtype=jnp.int32)[None, None, :]
    ).astype(jnp.float32)
    select = jnp.einsum("dkr,dkl->drl", rank_hot, local_hot)
    my_owner = lax.dynamic_index_in_dim(ref_owner, holder, 0, keepdims=False)
    my_rank = lax.dynamic_index_in_dim(ref_rank, holder, 0, keepdims=False)
    position = my_owner * capacity + my_rank
    payload = normed.reshape(blk_dev, CHB * seg_dev * WIN)
    outgoing = jnp.einsum(
        "drl,lx->drx", select.astype(jnp.bfloat16), payload, preferred_element_type=jnp.float32
    ).astype(jnp.bfloat16)
    incoming = lax.all_to_all(outgoing, "pair", split_axis=0, concat_axis=0, tiled=True)
    picked = jnp.take(
        incoming.reshape(pair_count * capacity, CHB * seg_dev * WIN), position, axis=0
    )
    picked_spectra = spectra(picked.reshape(refs, CHB, seg_dev, WIN), tables)
    paired = picked_spectra.reshape(pairs_dev, 2, CHB, seg_dev, 2 * half_bins)
    cross = cross_stack(paired[:, 0], paired[:, 1], keep, half_bins)
    partial_lags = to_lags(cross, inverse)
    lag_part = lax.psum_scatter(partial_lags, "lag", scatter_dimension=1, tiled=True)
    stacked = lax.psum_scatter(lag_part, "seg", scatter_dimension=0, tiled=True)
    return stacked * scale


N = 768
BINS = N // 2
MESH = pl.DeviceIdType.MESH


def lag_tables(scale):
    freq = (2 * np.arange(BINS) + 1).astype(np.int64)
    times = np.arange(WIN).astype(np.int64)
    angle = (times[:, None] * freq[None, :] % (2 * N)) * (math.pi / N)
    forward = np.concatenate([np.cos(angle), -np.sin(angle)], axis=1)
    shifts = np.arange(LAGS).astype(np.int64) - MAXLAG
    back = (freq[:, None] * shifts[None, :] % (2 * N)) * (math.pi / N)
    inverse = np.concatenate([np.cos(back), -np.sin(back)], axis=0) * (2.0 * scale / N)
    return forward.astype(jnp.bfloat16), inverse.astype(jnp.bfloat16)


def exchange_kernel(
    pair_count, seg_count, blk_dev, pairs_out, ch,
    x_hbm, slot_ref, pairs_ref, f_hbm, w_hbm, recv2,
    xv, yv, fv, wv, send1, recv1, spec, cross, send2,
    local_sems, ss1, rs1, ss2, rs2,
):
    n = pair_count * seg_count
    me = lax.axis_index("pair") * seg_count + lax.axis_index("seg")
    rows = blk_dev * ch

    def where(d):
        return {"pair": d // seg_count, "seg": d % seg_count}

    get_x = pltpu.make_async_copy(x_hbm, xv, local_sems.at[0])
    get_f = pltpu.make_async_copy(f_hbm, fv, local_sems.at[1])
    get_w = pltpu.make_async_copy(w_hbm, wv, local_sems.at[2])
    get_x.start()
    get_f.start()
    get_w.start()

    barrier = pltpu.get_barrier_semaphore()

    def greet(i, carry):
        pl.semaphore_signal(
            barrier, inc=1, device_id=where((me + 1 + i) % n), device_id_type=MESH
        )
        return carry

    lax.fori_loop(0, n - 1, greet, 0)

    ti = lax.broadcasted_iota(jnp.int32, (WIN, WIN), 0)
    tj = lax.broadcasted_iota(jnp.int32, (WIN, WIN), 1)
    band = jnp.where(jnp.abs(ti - tj) <= HALF, 1.0, 0.0).astype(jnp.bfloat16)
    t = lax.broadcasted_iota(jnp.int32, (1, WIN), 1)
    count = (jnp.minimum(t + HALF, WIN - 1) - jnp.maximum(t - HALF, 0) + 1).astype(jnp.float32)
    get_x.wait()
    x = xv[...]
    mag = jnp.abs(x)
    high = mag.astype(jnp.bfloat16)
    low = (mag - high.astype(jnp.float32)).astype(jnp.bfloat16)
    sums = jnp.dot(high, band, preferred_element_type=jnp.float32) + jnp.dot(
        low, band, preferred_element_type=jnp.float32
    )
    yv[...] = x / (sums / count + EPS)

    def regroup(d, carry):
        parts = [
            yv[pl.ds(pl.multiple_of(b * CHB + d * ch, ch), ch), :] for b in range(blk_dev)
        ]
        send1[d] = jnp.concatenate(parts, axis=0).astype(jnp.bfloat16)
        return carry

    lax.fori_loop(0, n, regroup, 0)
    pl.semaphore_wait(barrier, n - 1)

    def copy1(d, src):
        return pltpu.make_async_remote_copy(
            src_ref=send1.at[d], dst_ref=recv1.at[src], send_sem=ss1.at[d], recv_sem=rs1.at[src],
            device_id=where(d), device_id_type=MESH,
        )

    def copy2(d, src):
        return pltpu.make_async_remote_copy(
            src_ref=send2.at[d], dst_ref=recv2.at[src], send_sem=ss2.at[d], recv_sem=rs2.at[src],
            device_id=where(d), device_id_type=MESH,
        )

    def start1(i, carry):
        copy1((me + n // 2 + i + (i >= n // 2).astype(jnp.int32)) % n, me).start()
        return carry

    lax.fori_loop(0, n - 1, start1, 0)
    recv1[me] = send1[me]

    def arrive1(i, carry):
        src = (me + 1 + i) % n
        copy1(src, src).wait_recv()
        return carry

    get_f.wait()
    lax.fori_loop(0, n - 1, arrive1, 0)

    got = recv1[...].reshape(n * rows, WIN)
    full = jnp.dot(got, fv[...], preferred_element_type=jnp.float32)
    for p in range(pair_count):
        for s in range(seg_count):
            for b in range(blk_dev):
                at = (p * seg_count + s) * rows + b * ch
                spec[p * blk_dev + b, s] = full[at : at + ch]
    get_w.wait()

    group = n // 4
    first = me // group

    def one_pair(q):
        u = spec[slot_ref[pairs_ref[q, 0]]]
        v = spec[slot_ref[pairs_ref[q, 1]]]
        ur, ui, vr, vi = u[..., :BINS], u[..., BINS:], v[..., :BINS], v[..., BINS:]
        re = jnp.sum(ur * vr + ui * vi, axis=0)
        im = jnp.sum(ur * vi - ui * vr, axis=0)
        return jnp.concatenate([re, im], axis=1)

    step = 16 // ch

    def chunk(k, carry):
        c = (first + 2 + k) % 4
        for j in range(group * pairs_out // step):
            q = c * (group * pairs_out) + j * step
            cross[j * 16 : (j + 1) * 16, :] = jnp.concatenate(
                [one_pair(q + i) for i in range(step)], axis=0
            ).astype(jnp.bfloat16)
        lags = jnp.dot(cross[...], wv[...], preferred_element_type=jnp.float32)
        send2[pl.ds(c * group, group)] = lags.astype(jnp.bfloat16).reshape(
            group, pairs_out * ch, LAGS
        )
        for g in range(group):
            d = c * group + g

            @pl.when(d != me)
            def _():
                copy2(d, me).start()

        return carry

    lax.fori_loop(0, 4, chunk, 0)
    recv2[me] = send2[me]

    def arrive2(i, carry):
        src = (me + 1 + i) % n
        copy2(src, src).wait_recv()
        copy1(src, src).wait_send()
        copy2(src, src).wait_send()
        return carry

    lax.fori_loop(0, n - 1, arrive2, 0)


def layout_kernel(n, ch, r_ref, o_ref):
    for j in range(o_ref.shape[0]):
        part = r_ref[...].astype(jnp.float32)[:, j * ch : (j + 1) * ch, :]
        o_ref[j] = part.reshape(n * ch, LAGS).T


def channel_shards(strain, block_slot, pair_blocks):
    pair_count = lax.axis_size("pair")
    seg_count = lax.axis_size("seg")
    n = pair_count * seg_count
    blk_dev = strain.shape[0] // CHB
    nblk = block_slot.shape[0]
    pairs_out = pair_blocks.shape[0] // n
    ch = CHB // n
    rows = blk_dev * ch
    forward, inverse = lag_tables(1.0 / math.sqrt(seg_count * WIN))
    group = n // 4
    any_spec = pl.BlockSpec(memory_space=pl.ANY)
    smem = pl.BlockSpec(memory_space=pltpu.SMEM)
    parts = pl.pallas_call(
        functools.partial(exchange_kernel, pair_count, seg_count, blk_dev, pairs_out, ch),
        out_shape=jax.ShapeDtypeStruct((n, pairs_out * ch, LAGS), jnp.bfloat16),
        in_specs=[any_spec, smem, smem, any_spec, any_spec],
        out_specs=pl.BlockSpec(memory_space=pltpu.VMEM),
        scratch_shapes=[
            pltpu.VMEM((blk_dev * CHB, WIN), jnp.float32),
            pltpu.VMEM((blk_dev * CHB, WIN), jnp.float32),
            pltpu.VMEM(forward.shape, jnp.bfloat16),
            pltpu.VMEM(inverse.shape, jnp.bfloat16),
            pltpu.VMEM((n, rows, WIN), jnp.bfloat16),
            pltpu.VMEM((n, rows, WIN), jnp.bfloat16),
            pltpu.VMEM((nblk, seg_count, ch, N), jnp.float32),
            pltpu.VMEM((group * pairs_out * ch, N), jnp.bfloat16),
            pltpu.VMEM((n, pairs_out * ch, LAGS), jnp.bfloat16),
            pltpu.SemaphoreType.DMA((3,)),
            pltpu.SemaphoreType.DMA((n,)),
            pltpu.SemaphoreType.DMA((n,)),
            pltpu.SemaphoreType.DMA((n,)),
            pltpu.SemaphoreType.DMA((n,)),
        ],
        compiler_params=pltpu.CompilerParams(
            collective_id=0, has_side_effects=True, vmem_limit_bytes=32 * 1024 * 1024
        ),
        name="exchange",
    )(strain, block_slot, pair_blocks, jnp.asarray(forward), jnp.asarray(inverse))
    return pl.pallas_call(
        functools.partial(layout_kernel, n, ch),
        out_shape=jax.ShapeDtypeStruct((pairs_out, LAGS, CHB), jnp.float32),
        in_specs=[pl.BlockSpec(memory_space=pltpu.VMEM)],
        out_specs=pl.BlockSpec(memory_space=pltpu.VMEM),
        compiler_params=pltpu.CompilerParams(vmem_limit_bytes=32 * 1024 * 1024),
        name="layout",
    )(parts)


def fits_channels(mesh):
    n = mesh.shape["pair"] * mesh.shape["seg"]
    return mesh.shape["lag"] == 1 and n % 4 == 0 and CHB % n == 0 and CHB // n in (8, 16)


def solution(mesh):
    in_specs = (P(("grp", "pair"), "seg"), P("grp"), P("grp", None))
    out_specs = P(("grp", "pair", "seg"), "lag", None)

    def run(strain, block_slot, pair_blocks):
        one_segment = strain.shape[1] == WIN * mesh.shape["seg"]
        body = channel_shards if fits_channels(mesh) and one_segment else shards
        return jax.shard_map(
            body, mesh=mesh, in_specs=in_specs, out_specs=out_specs, check_vma=False
        )(strain, block_slot, pair_blocks)

    return run
```

```python
import functools
import math

import jax
import jax.numpy as jnp
import numpy as np
from jax import lax
from jax.experimental import pallas as pl
from jax.experimental.pallas import tpu as pltpu
from jax.sharding import PartitionSpec as P

CHB = 128
WIN = 512
MAXLAG = 200
HALF = 64
LAGS = 400


EPS = 1e-06


def make_tables(freq_part, lag_count):
    half_bins = WIN // lag_count
    length = 2 * WIN
    freq = freq_part * half_bins + jnp.arange(half_bins, dtype=jnp.int32)
    times = jnp.arange(WIN, dtype=jnp.int32)
    first_bin = freq == 0
    angle = (times[:, None] * freq[None, :] % length).astype(jnp.float32) * (2.0 * math.pi / length)
    alternate = (1 - 2 * (times % 2)).astype(jnp.float32)
    sine = jnp.where(first_bin[None, :], alternate[:, None], jnp.sin(angle))
    forward = jnp.concatenate([jnp.cos(angle), sine], axis=1)
    forward_high = forward.astype(jnp.bfloat16)
    forward_low = (forward - forward_high.astype(jnp.float32)).astype(jnp.bfloat16)
    shifts = jnp.arange(LAGS, dtype=jnp.int32) - MAXLAG
    back_angle = (freq[:, None] * shifts[None, :] % length).astype(jnp.float32) * (
        2.0 * math.pi / length
    )
    weight = jnp.where(first_bin, 1.0, 2.0).astype(jnp.float32)[:, None]
    upper = weight * jnp.cos(back_angle) / length
    lag_sign = (1 - 2 * (shifts % 2)).astype(jnp.float32)
    lower = jnp.where(
        first_bin[:, None], lag_sign[None, :] / length, -2.0 * jnp.sin(back_angle) / length
    )
    inverse = jnp.concatenate([upper, lower], axis=0)
    keep = (freq > 0).astype(jnp.float32)
    return ((forward_high, forward_low), inverse, keep)


def spectra(blocks, tables):
    high = jnp.einsum("bcst,tk->bcsk", blocks, tables[0], preferred_element_type=jnp.float32)
    low = jnp.einsum("bcst,tk->bcsk", blocks, tables[1], preferred_element_type=jnp.float32)
    return high + low


def cross_stack(first, second, keep, half_bins):
    first_re, first_im = (first[..., :half_bins], first[..., half_bins:])
    second_re, second_im = (second[..., :half_bins], second[..., half_bins:])
    real_part = first_re * second_re + keep * first_im * second_im
    imag_part = (
        keep * (first_im * second_re - first_re * second_im) + (1.0 - keep) * first_im * second_im
    )
    return jnp.sum(jnp.concatenate([real_part, imag_part], axis=-1), axis=2)


def to_lags(cross, inverse):
    return jnp.einsum("pck,kl->plc", cross, inverse, precision=lax.Precision.HIGHEST)


def shards(strain, block_slot, pair_blocks):
    pair_count = lax.axis_size("pair")
    seg_count = lax.axis_size("seg")
    lag_count = lax.axis_size("lag")
    holder = lax.axis_index("pair")
    freq_part = lax.axis_index("lag")
    blk_dev = strain.shape[0] // CHB
    seg_dev = strain.shape[1] // WIN
    nblk = block_slot.shape[0]
    pairs_dev = pair_blocks.shape[0] // pair_count
    refs = 2 * pairs_dev
    capacity = (refs + pair_count - 1) // pair_count
    half_bins = WIN // lag_count
    scale = 1.0 / math.sqrt(seg_dev * seg_count * WIN)
    series = strain.reshape(blk_dev, CHB, seg_dev, WIN)
    times = jnp.arange(WIN, dtype=jnp.int32)
    band = (jnp.abs(times[:, None] - times[None, :]) <= HALF).astype(jnp.float32)
    count = jnp.sum(band, axis=0)
    sums = jnp.einsum("bcst,tu->bcsu", jnp.abs(series), band, precision=lax.Precision.HIGHEST)
    normed = (series / (sums / count + EPS)).astype(jnp.bfloat16)
    tables, inverse, keep = make_tables(freq_part, lag_count)
    catalog = jnp.arange(nblk, dtype=jnp.int32)
    wanted = pair_blocks.reshape(pair_count, refs)
    hits = (wanted[:, :, None] == catalog[None, None, :]).astype(jnp.int32)
    ref_slot = jnp.sum(hits * block_slot[None, None, :], axis=2)
    ref_owner = ref_slot // blk_dev
    ref_local = ref_slot % blk_dev
    ordering = jnp.arange(refs, dtype=jnp.int32)
    earlier = ordering[:, None] > ordering[None, :]
    ref_rank = jnp.sum(
        ((ref_owner[:, :, None] == ref_owner[:, None, :]) & earlier[None, :, :]).astype(jnp.int32),
        axis=2,
    )
    mine = ref_owner == holder
    rank_hot = (
        (ref_rank[:, :, None] == jnp.arange(capacity, dtype=jnp.int32)[None, None, :])
        & mine[:, :, None]
    ).astype(jnp.float32)
    local_hot = (
        ref_local[:, :, None] == jnp.arange(blk_dev, dtype=jnp.int32)[None, None, :]
    ).astype(jnp.float32)
    select = jnp.einsum("dkr,dkl->drl", rank_hot, local_hot)
    my_owner = lax.dynamic_index_in_dim(ref_owner, holder, 0, keepdims=False)
    my_rank = lax.dynamic_index_in_dim(ref_rank, holder, 0, keepdims=False)
    position = my_owner * capacity + my_rank
    payload = normed.reshape(blk_dev, CHB * seg_dev * WIN)
    outgoing = jnp.einsum(
        "drl,lx->drx", select.astype(jnp.bfloat16), payload, preferred_element_type=jnp.float32
    ).astype(jnp.bfloat16)
    incoming = lax.all_to_all(outgoing, "pair", split_axis=0, concat_axis=0, tiled=True)
    picked = jnp.take(
        incoming.reshape(pair_count * capacity, CHB * seg_dev * WIN), position, axis=0
    )
    picked_spectra = spectra(picked.reshape(refs, CHB, seg_dev, WIN), tables)
    paired = picked_spectra.reshape(pairs_dev, 2, CHB, seg_dev, 2 * half_bins)
    cross = cross_stack(paired[:, 0], paired[:, 1], keep, half_bins)
    partial_lags = to_lags(cross, inverse)
    lag_part = lax.psum_scatter(partial_lags, "lag", scatter_dimension=1, tiled=True)
    stacked = lax.psum_scatter(lag_part, "seg", scatter_dimension=0, tiled=True)
    return stacked * scale


N = 768
BINS = N // 2
LANES = 128
BULK = LAGS // LANES * LANES
TAIL = LAGS - BULK
MESH = pl.DeviceIdType.MESH


def lag_tables(scale):
    freq = (2 * np.arange(BINS) + 1).astype(np.int64)
    times = np.arange(WIN).astype(np.int64)
    angle = (times[:, None] * freq[None, :] % (2 * N)) * (math.pi / N)
    forward = np.concatenate([np.cos(angle), -np.sin(angle)], axis=1)
    shifts = np.arange(LAGS).astype(np.int64) - MAXLAG
    back = (freq[:, None] * shifts[None, :] % (2 * N)) * (math.pi / N)
    inverse = np.concatenate([np.cos(back), -np.sin(back)], axis=0) * (2.0 * scale / N)
    tail = inverse[:, BULK:]
    blank = np.zeros((N, LANES - 2 * TAIL))
    inverse = np.concatenate([inverse, tail, blank], axis=1)
    return forward.astype(jnp.bfloat16), inverse.astype(jnp.bfloat16)


def exchange_kernel(
    pair_count, seg_count, blk_dev, pairs_out, ch,
    x_hbm, slot_hbm, pairs_hbm, f_hbm, w_hbm, recv2,
    xv, slot_ref, pairs_ref, fv, wv, band, send1, recv1, spec, cross, send2,
    local_sems, ss1, rs1, ss2, rs2,
):
    n = pair_count * seg_count
    me = lax.axis_index("pair") * seg_count + lax.axis_index("seg")
    rows = blk_dev * ch
    group = n // 4
    first = me // group

    def where(d):
        return {"pair": d // seg_count, "seg": d % seg_count}

    gets = [
        pltpu.make_async_copy(src, dst, local_sems.at[i])
        for i, (src, dst) in enumerate(
            [(x_hbm, xv), (f_hbm, fv), (w_hbm, wv), (slot_hbm, slot_ref), (pairs_hbm, pairs_ref)]
        )
    ]
    for get in gets:
        get.start()

    barrier = pltpu.get_barrier_semaphore()

    def greet(i, carry):
        pl.semaphore_signal(
            barrier, inc=1, device_id=where((me + 1 + i) % n), device_id_type=MESH
        )
        return carry

    lax.fori_loop(0, n - 1, greet, 0)

    def copy1(d, src):
        return pltpu.make_async_remote_copy(
            src_ref=send1.at[d], dst_ref=recv1.at[src], send_sem=ss1.at[d], recv_sem=rs1.at[src],
            device_id=where(d), device_id_type=MESH,
        )

    def copy2(d, src):
        return pltpu.make_async_remote_copy(
            src_ref=send2.at[d], dst_ref=recv2.at[src], send_sem=ss2.at[d], recv_sem=rs2.at[src],
            device_id=where(d), device_id_type=MESH,
        )

    def quarter(k):
        high = (first // 2 + jnp.where(k < 2, 1, 0)) % 2
        low = (first + jnp.where((k == 1) | (k == 2), 1, 0)) % 2
        return 2 * high + low

    ti = lax.broadcasted_iota(jnp.int32, (WIN, WIN), 0)
    tj = lax.broadcasted_iota(jnp.int32, (WIN, WIN), 1)
    band[...] = jnp.where(jnp.abs(ti - tj) <= HALF, 1.0, 0.0).astype(jnp.bfloat16)
    t = lax.broadcasted_iota(jnp.int32, (1, WIN), 1)
    count = (jnp.minimum(t + HALF, WIN - 1) - jnp.maximum(t - HALF, 0) + 1).astype(jnp.float32)
    gets[0].wait()

    for k in range(4):
        c = quarter(k)
        span = group * ch
        x = jnp.concatenate(
            [xv[pl.ds(pl.multiple_of(b * CHB + c * span, span), span), :] for b in range(blk_dev)],
            axis=0,
        )
        mag = jnp.abs(x)
        high = mag.astype(jnp.bfloat16)
        low = (mag - high.astype(jnp.float32)).astype(jnp.bfloat16)
        sums = jnp.dot(high, band[...], preferred_element_type=jnp.float32) + jnp.dot(
            low, band[...], preferred_element_type=jnp.float32
        )
        y = x / (sums / count + EPS)
        for g in range(group):
            part = [y[b * span + g * ch : b * span + (g + 1) * ch] for b in range(blk_dev)]
            send1[c * group + g] = jnp.concatenate(part, axis=0).astype(jnp.bfloat16)
        if k == 0:
            pl.semaphore_wait(barrier, n - 1)
        for g in range(group):
            d = c * group + g

            @pl.when(d != me)
            def _():
                copy1(d, me).start()

    recv1[me] = send1[me]
    gets[1].wait()

    for k in (3, 2, 1, 0):
        c = quarter(k)
        for g in range(group):
            src = c * group + g

            @pl.when(src != me)
            def _():
                copy1(src, src).wait_recv()

        got = recv1[pl.ds(c * group, group)].reshape(group * rows, WIN)
        full = jnp.dot(got, fv[...], preferred_element_type=jnp.float32)
        for g in range(group):
            p = c * (group // seg_count) + g // seg_count
            for b in range(blk_dev):
                at = g * rows + b * ch
                spec[p * blk_dev + b, g % seg_count] = full[at : at + ch]
    for get in gets[2:]:
        get.wait()

    def one_pair(q):
        u = spec[slot_ref[pairs_ref[0, q]]]
        v = spec[slot_ref[pairs_ref[1, q]]]
        ur, ui, vr, vi = u[..., :BINS], u[..., BINS:], v[..., :BINS], v[..., BINS:]
        re = jnp.sum(ur * vr + ui * vi, axis=0)
        im = jnp.sum(ur * vi - ui * vr, axis=0)
        return jnp.concatenate([re, im], axis=1)

    step = 16 // ch
    size = pairs_out * ch

    def chunk(k, carry):
        c = quarter(k)
        for j in range(group * pairs_out // step):
            q = c * (group * pairs_out) + j * step
            cross[j * 16 : (j + 1) * 16, :] = jnp.concatenate(
                [one_pair(q + i) for i in range(step)], axis=0
            ).astype(jnp.bfloat16)
        lags = jnp.dot(cross[...], wv[...], preferred_element_type=jnp.float32)
        for g in range(group):
            d = c * group + g
            mine = lags[g * size : (g + 1) * size]
            for m in range(BULK // LANES):
                send2[d, m * size : (m + 1) * size, :] = mine[
                    :, m * LANES : (m + 1) * LANES
                ].astype(jnp.bfloat16)
            rest = mine[:, BULK:]
            lane = lax.broadcasted_iota(jnp.int32, (size // 2, LANES), 1)
            send2[d, BULK // LANES * size :, :] = jnp.where(
                lane < TAIL, rest[: size // 2], rest[size // 2 :]
            ).astype(jnp.bfloat16)

            @pl.when(d != me)
            def _():
                copy2(d, me).start()

        return carry

    lax.fori_loop(0, 4, chunk, 0)
    recv2[me] = send2[me]

    def arrive2(i, carry):
        src = (me + 1 + i) % n
        copy2(src, src).wait_recv()
        copy1(src, src).wait_send()
        copy2(src, src).wait_send()
        return carry

    lax.fori_loop(0, n - 1, arrive2, 0)


def layout_kernel(n, ch, r_ref, o_hbm, ov, sems):
    pairs_out = ov.shape[0]
    size = pairs_out * ch
    tiles = BULK // LANES

    def turned(row):
        return r_ref[:, row : row + ch, :].astype(jnp.float32).reshape(n * ch, LANES).T

    half = pairs_out // 2
    for j in range(half):
        rest = turned(tiles * size + j * ch)
        for i, p in enumerate((j, j + half)):
            for m in range(tiles):
                ov[p, m * LANES : (m + 1) * LANES, :] = turned(m * size + p * ch)
            ov[p, BULK:, :] = rest[i * TAIL : (i + 1) * TAIL]
            pltpu.make_async_copy(ov.at[p], o_hbm.at[p], sems.at[p]).start()
    for p in range(pairs_out):
        pltpu.make_async_copy(ov.at[p], o_hbm.at[p], sems.at[p]).wait()


def channel_shards(strain, block_slot, pair_blocks):
    pair_count = lax.axis_size("pair")
    seg_count = lax.axis_size("seg")
    n = pair_count * seg_count
    blk_dev = strain.shape[0] // CHB
    nblk = block_slot.shape[0]
    pairs_out = pair_blocks.shape[0] // n
    ch = CHB // n
    rows = blk_dev * ch
    message = pairs_out * ch // 2 * (2 * BULK // LANES + 1)
    forward, inverse = lag_tables(1.0 / math.sqrt(seg_count * WIN))
    group = n // 4
    any_spec = pl.BlockSpec(memory_space=pl.ANY)
    parts = pl.pallas_call(
        functools.partial(exchange_kernel, pair_count, seg_count, blk_dev, pairs_out, ch),
        out_shape=jax.ShapeDtypeStruct((n, message, LANES), jnp.bfloat16),
        in_specs=[any_spec] * 5,
        out_specs=pl.BlockSpec(memory_space=pltpu.VMEM),
        scratch_shapes=[
            pltpu.VMEM((blk_dev * CHB, WIN), jnp.float32),
            pltpu.SMEM((nblk,), jnp.int32),
            pltpu.SMEM((2, pair_blocks.shape[0]), jnp.int32),
            pltpu.VMEM(forward.shape, jnp.bfloat16),
            pltpu.VMEM(inverse.shape, jnp.bfloat16),
            pltpu.VMEM((WIN, WIN), jnp.bfloat16),
            pltpu.VMEM((n, rows, WIN), jnp.bfloat16),
            pltpu.VMEM((n, rows, WIN), jnp.bfloat16),
            pltpu.VMEM((nblk, seg_count, ch, N), jnp.float32),
            pltpu.VMEM((group * pairs_out * ch, N), jnp.bfloat16),
            pltpu.VMEM((n, message, LANES), jnp.bfloat16),
            pltpu.SemaphoreType.DMA((5,)),
            pltpu.SemaphoreType.DMA((n,)),
            pltpu.SemaphoreType.DMA((n,)),
            pltpu.SemaphoreType.DMA((n,)),
            pltpu.SemaphoreType.DMA((n,)),
        ],
        compiler_params=pltpu.CompilerParams(
            collective_id=0, has_side_effects=True, vmem_limit_bytes=62 * 1024 * 1024
        ),
        name="exchange",
    )(strain, block_slot, pair_blocks.T, jnp.asarray(forward), jnp.asarray(inverse))
    return pl.pallas_call(
        functools.partial(layout_kernel, n, ch),
        out_shape=jax.ShapeDtypeStruct((pairs_out, LAGS, CHB), jnp.float32),
        in_specs=[pl.BlockSpec(memory_space=pltpu.VMEM)],
        out_specs=any_spec,
        scratch_shapes=[
            pltpu.VMEM((pairs_out, LAGS, CHB), jnp.float32),
            pltpu.SemaphoreType.DMA((pairs_out,)),
        ],
        compiler_params=pltpu.CompilerParams(vmem_limit_bytes=32 * 1024 * 1024),
        name="layout",
    )(parts)


def fits_channels(mesh):
    n = mesh.shape["pair"] * mesh.shape["seg"]
    whole = n % (4 * mesh.shape["seg"]) == 0 and CHB % n == 0
    return mesh.shape["lag"] == 1 and whole and CHB // n in (8, 16)


def solution(mesh):
    in_specs = (P(("grp", "pair"), "seg"), P("grp"), P("grp", None))
    out_specs = P(("grp", "pair", "seg"), "lag", None)

    def run(strain, block_slot, pair_blocks):
        one_segment = strain.shape[1] == WIN * mesh.shape["seg"]
        body = channel_shards if fits_channels(mesh) and one_segment else shards
        return jax.shard_map(
            body, mesh=mesh, in_specs=in_specs, out_specs=out_specs, check_vma=False
        )(strain, block_slot, pair_blocks)

    return run
```

```python
import functools
import math

import jax
import jax.numpy as jnp
import numpy as np
from jax import lax
from jax.experimental import pallas as pl
from jax.experimental.pallas import tpu as pltpu
from jax.sharding import PartitionSpec as P

CHB = 128
WIN = 512
MAXLAG = 200
HALF = 64
LAGS = 400


EPS = 1e-06


def make_tables(freq_part, lag_count):
    half_bins = WIN // lag_count
    length = 2 * WIN
    freq = freq_part * half_bins + jnp.arange(half_bins, dtype=jnp.int32)
    times = jnp.arange(WIN, dtype=jnp.int32)
    first_bin = freq == 0
    angle = (times[:, None] * freq[None, :] % length).astype(jnp.float32) * (2.0 * math.pi / length)
    alternate = (1 - 2 * (times % 2)).astype(jnp.float32)
    sine = jnp.where(first_bin[None, :], alternate[:, None], jnp.sin(angle))
    forward = jnp.concatenate([jnp.cos(angle), sine], axis=1)
    forward_high = forward.astype(jnp.bfloat16)
    forward_low = (forward - forward_high.astype(jnp.float32)).astype(jnp.bfloat16)
    shifts = jnp.arange(LAGS, dtype=jnp.int32) - MAXLAG
    back_angle = (freq[:, None] * shifts[None, :] % length).astype(jnp.float32) * (
        2.0 * math.pi / length
    )
    weight = jnp.where(first_bin, 1.0, 2.0).astype(jnp.float32)[:, None]
    upper = weight * jnp.cos(back_angle) / length
    lag_sign = (1 - 2 * (shifts % 2)).astype(jnp.float32)
    lower = jnp.where(
        first_bin[:, None], lag_sign[None, :] / length, -2.0 * jnp.sin(back_angle) / length
    )
    inverse = jnp.concatenate([upper, lower], axis=0)
    keep = (freq > 0).astype(jnp.float32)
    return ((forward_high, forward_low), inverse, keep)


def spectra(blocks, tables):
    high = jnp.einsum("bcst,tk->bcsk", blocks, tables[0], preferred_element_type=jnp.float32)
    low = jnp.einsum("bcst,tk->bcsk", blocks, tables[1], preferred_element_type=jnp.float32)
    return high + low


def cross_stack(first, second, keep, half_bins):
    first_re, first_im = (first[..., :half_bins], first[..., half_bins:])
    second_re, second_im = (second[..., :half_bins], second[..., half_bins:])
    real_part = first_re * second_re + keep * first_im * second_im
    imag_part = (
        keep * (first_im * second_re - first_re * second_im) + (1.0 - keep) * first_im * second_im
    )
    return jnp.sum(jnp.concatenate([real_part, imag_part], axis=-1), axis=2)


def to_lags(cross, inverse):
    return jnp.einsum("pck,kl->plc", cross, inverse, precision=lax.Precision.HIGHEST)


def shards(strain, block_slot, pair_blocks):
    pair_count = lax.axis_size("pair")
    seg_count = lax.axis_size("seg")
    lag_count = lax.axis_size("lag")
    holder = lax.axis_index("pair")
    freq_part = lax.axis_index("lag")
    blk_dev = strain.shape[0] // CHB
    seg_dev = strain.shape[1] // WIN
    nblk = block_slot.shape[0]
    pairs_dev = pair_blocks.shape[0] // pair_count
    refs = 2 * pairs_dev
    capacity = (refs + pair_count - 1) // pair_count
    half_bins = WIN // lag_count
    scale = 1.0 / math.sqrt(seg_dev * seg_count * WIN)
    series = strain.reshape(blk_dev, CHB, seg_dev, WIN)
    times = jnp.arange(WIN, dtype=jnp.int32)
    band = (jnp.abs(times[:, None] - times[None, :]) <= HALF).astype(jnp.float32)
    count = jnp.sum(band, axis=0)
    sums = jnp.einsum("bcst,tu->bcsu", jnp.abs(series), band, precision=lax.Precision.HIGHEST)
    normed = (series / (sums / count + EPS)).astype(jnp.bfloat16)
    tables, inverse, keep = make_tables(freq_part, lag_count)
    catalog = jnp.arange(nblk, dtype=jnp.int32)
    wanted = pair_blocks.reshape(pair_count, refs)
    hits = (wanted[:, :, None] == catalog[None, None, :]).astype(jnp.int32)
    ref_slot = jnp.sum(hits * block_slot[None, None, :], axis=2)
    ref_owner = ref_slot // blk_dev
    ref_local = ref_slot % blk_dev
    ordering = jnp.arange(refs, dtype=jnp.int32)
    earlier = ordering[:, None] > ordering[None, :]
    ref_rank = jnp.sum(
        ((ref_owner[:, :, None] == ref_owner[:, None, :]) & earlier[None, :, :]).astype(jnp.int32),
        axis=2,
    )
    mine = ref_owner == holder
    rank_hot = (
        (ref_rank[:, :, None] == jnp.arange(capacity, dtype=jnp.int32)[None, None, :])
        & mine[:, :, None]
    ).astype(jnp.float32)
    local_hot = (
        ref_local[:, :, None] == jnp.arange(blk_dev, dtype=jnp.int32)[None, None, :]
    ).astype(jnp.float32)
    select = jnp.einsum("dkr,dkl->drl", rank_hot, local_hot)
    my_owner = lax.dynamic_index_in_dim(ref_owner, holder, 0, keepdims=False)
    my_rank = lax.dynamic_index_in_dim(ref_rank, holder, 0, keepdims=False)
    position = my_owner * capacity + my_rank
    payload = normed.reshape(blk_dev, CHB * seg_dev * WIN)
    outgoing = jnp.einsum(
        "drl,lx->drx", select.astype(jnp.bfloat16), payload, preferred_element_type=jnp.float32
    ).astype(jnp.bfloat16)
    incoming = lax.all_to_all(outgoing, "pair", split_axis=0, concat_axis=0, tiled=True)
    picked = jnp.take(
        incoming.reshape(pair_count * capacity, CHB * seg_dev * WIN), position, axis=0
    )
    picked_spectra = spectra(picked.reshape(refs, CHB, seg_dev, WIN), tables)
    paired = picked_spectra.reshape(pairs_dev, 2, CHB, seg_dev, 2 * half_bins)
    cross = cross_stack(paired[:, 0], paired[:, 1], keep, half_bins)
    partial_lags = to_lags(cross, inverse)
    lag_part = lax.psum_scatter(partial_lags, "lag", scatter_dimension=1, tiled=True)
    stacked = lax.psum_scatter(lag_part, "seg", scatter_dimension=0, tiled=True)
    return stacked * scale


N = 768
BINS = N // 2
LANES = 128
BULK = LAGS // LANES * LANES
TAIL = LAGS - BULK
MESH = pl.DeviceIdType.MESH


def lag_tables(scale):
    freq = (2 * np.arange(BINS) + 1).astype(np.int64)
    times = np.arange(WIN).astype(np.int64)
    angle = (times[:, None] * freq[None, :] % (2 * N)) * (math.pi / N)
    forward = np.concatenate([np.cos(angle), -np.sin(angle)], axis=1)
    shifts = np.arange(LAGS).astype(np.int64) - MAXLAG
    back = (freq[:, None] * shifts[None, :] % (2 * N)) * (math.pi / N)
    inverse = np.concatenate([np.cos(back), -np.sin(back)], axis=0) * (2.0 * scale / N)
    tail = inverse[:, BULK:]
    blank = np.zeros((N, LANES - 2 * TAIL))
    inverse = np.concatenate([inverse, tail, blank], axis=1)
    return forward.astype(jnp.bfloat16), inverse.astype(jnp.bfloat16)


def exchange_kernel(
    pair_count, seg_count, blk_dev, pairs_out, ch,
    x_hbm, slot_hbm, pairs_hbm, f_hbm, w_hbm, recv2,
    xv, slot_ref, pairs_ref, fv, wv, band, send1, recv1, spec, cross, send2,
    local_sems, ss1, rs1, ss2, rs2,
):
    n = pair_count * seg_count
    me = lax.axis_index("pair") * seg_count + lax.axis_index("seg")
    rows = blk_dev * ch
    group = n // 4
    half = n // 2
    first = me // group
    side, place = me // half, me % half
    size = pairs_out * ch

    def where(d):
        return {"pair": d // seg_count, "seg": d % seg_count}

    gets = [
        pltpu.make_async_copy(src, dst, local_sems.at[i])
        for i, (src, dst) in enumerate(
            [(x_hbm, xv), (f_hbm, fv), (w_hbm, wv), (slot_hbm, slot_ref), (pairs_hbm, pairs_ref)]
        )
    ]
    for get in gets:
        get.start()

    barrier = pltpu.get_barrier_semaphore()

    def greet(i, carry):
        pl.semaphore_signal(
            barrier, inc=1, device_id=where((me + 1 + i) % n), device_id_type=MESH
        )
        return carry

    lax.fori_loop(0, n - 1, greet, 0)

    def copy1(r, d, src):
        return pltpu.make_async_remote_copy(
            src_ref=send1.at[r * half + d % half], dst_ref=recv1.at[r * n + src],
            send_sem=ss1.at[r * n + d], recv_sem=rs1.at[r * n + src],
            device_id=where(d), device_id_type=MESH,
        )

    def copy2(r, d, src):
        return pltpu.make_async_remote_copy(
            src_ref=send2.at[r * half + d % half], dst_ref=recv2.at[src % half * 2 + r],
            send_sem=ss2.at[r * half + d % half], recv_sem=rs2.at[src % half * 2 + r],
            device_id=where(d), device_id_type=MESH,
        )

    def quarter(k):
        high = (first // 2 + jnp.where(k < 2, 1, 0)) % 2
        low = (first + jnp.where((k == 1) | (k == 2), 1, 0)) % 2
        return 2 * high + low

    ti = lax.broadcasted_iota(jnp.int32, (WIN, WIN), 0)
    tj = lax.broadcasted_iota(jnp.int32, (WIN, WIN), 1)
    band[...] = jnp.where(jnp.abs(ti - tj) <= HALF, 1.0, 0.0).astype(jnp.bfloat16)
    t = lax.broadcasted_iota(jnp.int32, (1, WIN), 1)
    count = (jnp.minimum(t + HALF, WIN - 1) - jnp.maximum(t - HALF, 0) + 1).astype(jnp.float32)
    gets[0].wait()

    span = half * ch
    for m in range(2):
        x = jnp.concatenate(
            [xv[b * CHB + m * span : b * CHB + (m + 1) * span, :] for b in range(blk_dev)], axis=0
        )
        mag = jnp.abs(x)
        high = mag.astype(jnp.bfloat16)
        low = (mag - high.astype(jnp.float32)).astype(jnp.bfloat16)
        sums = jnp.dot(high, band[...], preferred_element_type=jnp.float32) + jnp.dot(
            low, band[...], preferred_element_type=jnp.float32
        )
        y = x / (sums / count + EPS)
        for g in range(group):
            for r in range(2):
                at = (2 * g + r) * ch
                part = [y[b * span + at : b * span + at + ch] for b in range(blk_dev)]
                send1[r * half + m * group + g] = jnp.concatenate(part, axis=0).astype(jnp.bfloat16)
    pl.semaphore_wait(barrier, n - 1)

    for r in range(2):

        def across(i, carry):
            copy1(r, (1 - side) * half + (place + i) % half, me).start()
            return carry

        def beside(i, carry):
            copy1(r, side * half + (place + 1 + i) % half, me).start()
            return carry

        lax.fori_loop(0, half, across, 0)
        lax.fori_loop(0, half - 1, beside, 0)
        recv1[r * n + me] = send1[r * half + place]
    for get in gets[1:]:
        get.wait()

    def one_pair(q):
        u = spec[slot_ref[pairs_ref[0, q]]]
        v = spec[slot_ref[pairs_ref[1, q]]]
        ur, ui, vr, vi = u[..., :BINS], u[..., BINS:], v[..., :BINS], v[..., BINS:]
        re = jnp.sum(ur * vr + ui * vi, axis=0)
        im = jnp.sum(ur * vi - ui * vr, axis=0)
        return jnp.concatenate([re, im], axis=1)

    step = 16 // ch

    for r in range(2):
        for k in (3, 2, 1, 0):
            c = quarter(k)
            for g in range(group):
                src = c * group + g

                @pl.when(src != me)
                def _():
                    copy1(r, src, src).wait_recv()

            got = recv1[pl.ds(r * n + c * group, group)].reshape(group * rows, WIN)
            full = jnp.dot(got, fv[...], preferred_element_type=jnp.float32)
            for g in range(group):
                p = c * (group // seg_count) + g // seg_count
                for b in range(blk_dev):
                    at = g * rows + b * ch
                    spec[p * blk_dev + b, g % seg_count] = full[at : at + ch]

        def chunk(k, carry):
            c = quarter(k)
            for j in range(group * pairs_out // step):
                q = c * (group * pairs_out) + j * step
                cross[j * 16 : (j + 1) * 16, :] = jnp.concatenate(
                    [one_pair(q + i) for i in range(step)], axis=0
                ).astype(jnp.bfloat16)
            lags = jnp.dot(cross[...], wv[...], preferred_element_type=jnp.float32)
            lane = lax.broadcasted_iota(jnp.int32, (size // 2, LANES), 1)
            for g in range(group):
                d = c * group + g
                to = r * half + d % half
                mine = lags[g * size : (g + 1) * size]
                for m in range(BULK // LANES):
                    send2[to, m * size : (m + 1) * size, :] = mine[
                        :, m * LANES : (m + 1) * LANES
                    ].astype(jnp.bfloat16)
                rest = mine[:, BULK:]
                send2[to, BULK // LANES * size :, :] = jnp.where(
                    lane < TAIL, rest[: size // 2], rest[size // 2 :]
                ).astype(jnp.bfloat16)

                @pl.when(d != me)
                def _():
                    copy2(r, d, me).start()

            return carry

        lax.fori_loop(2, 4, chunk, 0)
        recv2[place * 2 + r] = send2[r * half + place]

    for r in range(2):

        def arrive2(i, carry):
            src = side * half + (place + 1 + i) % half
            copy2(r, src, src).wait_recv()
            copy2(r, src, src).wait_send()
            return carry

        def sent1(i, carry):
            copy1(r, (me + 1 + i) % n, me).wait_send()
            return carry

        lax.fori_loop(0, half - 1, arrive2, 0)
        lax.fori_loop(0, n - 1, sent1, 0)


def layout_kernel(n, ch, r_ref, o_hbm, ov, sems):
    pairs_out = ov.shape[0]
    size = pairs_out * ch
    tiles = BULK // LANES

    def turned(row):
        return r_ref[:, row : row + ch, :].astype(jnp.float32).reshape(n * ch, LANES).T

    half = pairs_out // 2
    for j in range(half):
        rest = turned(tiles * size + j * ch)
        for i, p in enumerate((j, j + half)):
            for m in range(tiles):
                ov[p, m * LANES : (m + 1) * LANES, :] = turned(m * size + p * ch)
            ov[p, BULK:, :] = rest[i * TAIL : (i + 1) * TAIL]
            pltpu.make_async_copy(ov.at[p], o_hbm.at[p], sems.at[p]).start()
    for p in range(pairs_out):
        pltpu.make_async_copy(ov.at[p], o_hbm.at[p], sems.at[p]).wait()


def channel_shards(strain, block_slot, pair_blocks):
    pair_count = lax.axis_size("pair")
    seg_count = lax.axis_size("seg")
    n = pair_count * seg_count
    blk_dev = strain.shape[0] // CHB
    nblk = block_slot.shape[0]
    pairs_out = pair_blocks.shape[0] // n
    ch = CHB // n
    rows = blk_dev * ch
    message = pairs_out * ch // 2 * (2 * BULK // LANES + 1)
    forward, inverse = lag_tables(1.0 / math.sqrt(seg_count * WIN))
    group = n // 4
    any_spec = pl.BlockSpec(memory_space=pl.ANY)
    parts = pl.pallas_call(
        functools.partial(exchange_kernel, pair_count, seg_count, blk_dev, pairs_out, ch),
        out_shape=pltpu.VMEM((n, message, LANES), jnp.bfloat16),
        in_specs=[any_spec] * 5,
        out_specs=pl.BlockSpec(memory_space=pltpu.VMEM),
        scratch_shapes=[
            pltpu.VMEM((blk_dev * CHB, WIN), jnp.float32),
            pltpu.SMEM((nblk,), jnp.int32),
            pltpu.SMEM((2, pair_blocks.shape[0]), jnp.int32),
            pltpu.VMEM(forward.shape, jnp.bfloat16),
            pltpu.VMEM(inverse.shape, jnp.bfloat16),
            pltpu.VMEM((WIN, WIN), jnp.bfloat16),
            pltpu.VMEM((n, rows, WIN), jnp.bfloat16),
            pltpu.VMEM((2 * n, rows, WIN), jnp.bfloat16),
            pltpu.VMEM((nblk, seg_count, ch, N), jnp.float32),
            pltpu.VMEM((group * pairs_out * ch, N), jnp.bfloat16),
            pltpu.VMEM((n, message, LANES), jnp.bfloat16),
            pltpu.SemaphoreType.DMA((5,)),
            pltpu.SemaphoreType.DMA((2 * n,)),
            pltpu.SemaphoreType.DMA((2 * n,)),
            pltpu.SemaphoreType.DMA((n,)),
            pltpu.SemaphoreType.DMA((n,)),
        ],
        compiler_params=pltpu.CompilerParams(
            collective_id=0, has_side_effects=True, vmem_limit_bytes=62 * 1024 * 1024
        ),
        name="exchange",
    )(strain, block_slot, pair_blocks.T, jnp.asarray(forward), jnp.asarray(inverse))
    return pl.pallas_call(
        functools.partial(layout_kernel, n, ch),
        out_shape=jax.ShapeDtypeStruct((pairs_out, LAGS, CHB), jnp.float32),
        in_specs=[pl.BlockSpec(memory_space=pltpu.VMEM)],
        out_specs=any_spec,
        scratch_shapes=[
            pltpu.VMEM((pairs_out, LAGS, CHB), jnp.float32),
            pltpu.SemaphoreType.DMA((pairs_out,)),
        ],
        compiler_params=pltpu.CompilerParams(vmem_limit_bytes=32 * 1024 * 1024),
        name="layout",
    )(parts)


def fits_channels(mesh):
    n = mesh.shape["pair"] * mesh.shape["seg"]
    whole = n % (4 * mesh.shape["seg"]) == 0 and CHB % n == 0
    return mesh.shape["lag"] == 1 and whole and CHB // n in (8, 16)


def solution(mesh):
    in_specs = (P(("grp", "pair"), "seg"), P("grp"), P("grp", None))
    out_specs = P(("grp", "pair", "seg"), "lag", None)

    def run(strain, block_slot, pair_blocks):
        one_segment = strain.shape[1] == WIN * mesh.shape["seg"]
        body = channel_shards if fits_channels(mesh) and one_segment else shards
        return jax.shard_map(
            body, mesh=mesh, in_specs=in_specs, out_specs=out_specs, check_vma=False
        )(strain, block_slot, pair_blocks)

    return run
```
